32 devices in a mesh: groups: 2 (over x), row: 8 (over z, y), col: 2 (over core).
Axes of the slice: x: 2, y: 2, z: 4, core: 2. Of those that a mesh axis runs over, the one named last changes fastest.
Arguments:
- features: bfloat16 [32, 8, 256, 1024], P(('groups', 'row'), 'col'), parts along dimension 0, may hold values from -6 to 6
- assignment: int32 [32, 8], P(('groups', 'row'), 'col'), parts along dimension 0, may hold values from -1 to 7, as said below
- w_reduce: bfloat16 [1024, 512], replicated, may hold values from -0.1875 to 0.1875
- w_expand: bfloat16 [512, 2048], replicated, may hold values from -0.25 to 0.25
- w_short: bfloat16 [1024, 2048], replicated, may hold values from -0.1875 to 0.1875
- w_branch: bfloat16 [2048, 256], replicated, may hold values from -0.125 to 0.125
- w_dilated: bfloat16 [9, 256, 256], replicated, may hold values from -0.125 to 0.125
Outputs:
- branch_out: bfloat16 [512, 128, 256], P(('groups', 'row'), 'col'), parts along dimension 0
The draws below stay inside these ranges and needn't reach their ends.
There are 2 independent parts, one for each index of `groups`. The reference program is written for one: setup_inputs(seed, part) draws one part's arguments, and reference() takes and returns one part's arrays. A program takes and returns all parts, laid end to end along the dimension named above; an argument that names none is the same for every part. Nothing has to cross between parts.
Inputs may be any that keep to these rules, and one draw needn't show every extreme that they name: `assignment`: A value v >= 0 means the tile has tissue and is handled in slot v % 4 by the worker of the same column index whose row index is the holder's row index XOR (v // 4): the holder itself for v < 4, else its partner. Each worker handles exactly 4 tiles, one in each slot, the holder's own tissue tiles included. In every column index some device's tiles are all tissue, so that it hands 4 tiles to its partner, and that partner holds none.
All inputs are finite; a program needn't handle non-finite values.
Results may differ from the reference program's by a relative error of at most 0.0061.
Values may be sent and summed in bfloat16 or wider, within the bound.
A program may use at most 64 MiB of HBM per device.

```python
import jax
import jax.numpy as jnp
from jax import lax

CIN = 1024
MID = 512
COUT = 2048
BR = 256
TILE = 16
TRD = 2
TCD = 4
RR = 18
RC = 15
LOAD = 4
TR = 16
TC = 8
N_ROW = 8
N_COL = 2


def draw_assignment(key, part):
    tile_count = TRD * TCD
    pair_count = N_ROW // 2
    spread = jax.random.randint(jax.random.fold_in(key, 11), (N_COL, pair_count), (LOAD + 1) // 2, LOAD + 1)
    spread = spread.at[:, 0].set(LOAD)
    flipped = jax.random.randint(jax.random.fold_in(key, 14), (N_COL, pair_count), 0, 2)
    higher = LOAD + spread
    lower = LOAD - spread
    even_count = jnp.where(flipped == 0, higher, lower)
    odd_count = jnp.where(flipped == 0, lower, higher)
    counts = jnp.stack([even_count, odd_count], axis=-1).reshape(N_COL, N_ROW)
    partner_counts = jnp.stack([odd_count, even_count], axis=-1).reshape(N_COL, N_ROW)
    rank_keys = jax.random.split(jax.random.fold_in(key, 13), N_COL * N_ROW)
    tile_ranks = jax.vmap(lambda single: jax.random.permutation(single, tile_count))(rank_keys)
    tile_ranks = tile_ranks.reshape(N_COL, N_ROW, tile_count).astype(jnp.int32)
    slot_keys = jax.random.split(jax.random.fold_in(key, 15), N_COL * N_ROW)
    slot_perms = jax.vmap(lambda single: jax.random.permutation(single, LOAD))(slot_keys)
    slot_perms = slot_perms.reshape(N_COL, N_ROW, LOAD).astype(jnp.int32)
    partner_perms = slot_perms.reshape(N_COL, pair_count, 2, LOAD)[:, :, ::-1, :].reshape(N_COL, N_ROW, LOAD)
    tissue = tile_ranks < counts[:, :, None]
    handed = tile_ranks >= LOAD
    base_slot = jnp.where(handed, partner_counts[:, :, None] + tile_ranks - LOAD, tile_ranks)
    base_slot = jnp.clip(base_slot, 0, LOAD - 1).astype(jnp.int32)
    own_slot = jnp.take_along_axis(slot_perms, base_slot, axis=2)
    other_slot = jnp.take_along_axis(partner_perms, base_slot, axis=2)
    slot_index = jnp.where(handed, other_slot, own_slot)
    values = jnp.where(tissue, handed.astype(jnp.int32) * LOAD + slot_index, -1).astype(jnp.int32)
    values = values.reshape(N_COL, N_ROW, TRD, TCD).transpose(1, 2, 0, 3)
    return values.reshape(TRD * N_ROW, TCD * N_COL)


def steps_of(key, extent, cuts, low, high):
    level, own = 1.0, jax.random.fold_in(key, 6)
    for axis_at, parts in cuts:
        draws = jnp.exp(jax.random.uniform(jax.random.fold_in(own, axis_at), (parts,), jnp.float32, low / len(cuts), high / len(cuts)))
        level = level * jnp.repeat(draws, extent[axis_at] // parts).reshape([-1 if axis == axis_at else 1 for axis in range(len(extent))])
    return level


def bell_draw(key, extent, scale, most, cuts=(), held_as=jnp.bfloat16):
    level = steps_of(key, extent, cuts, -0.22, 0.18) if cuts else 1.0
    result = jax.random.normal(key, extent, jnp.float32) * scale * level
    return jnp.minimum(jnp.maximum(result, -most), most).astype(held_as)


def setup_inputs(seed: int = 0, part: int = 0) -> dict:
    keys = jax.random.split(jax.random.key(seed), 8)
    part_splits = jax.random.split(jax.random.fold_in(keys[7], part), 8)
    features = bell_draw(part_splits[0], (TR, TC, TILE * TILE, CIN), 1.0, 6.0, ((0, 8), (1, 2)))
    assignment = draw_assignment(jax.random.fold_in(jax.random.fold_in(keys[7], part), 71), part)
    w_reduce = bell_draw(keys[2], (CIN, MID), CIN ** -0.5, 0.1875)
    w_expand = bell_draw(keys[3], (MID, COUT), MID ** -0.5, 0.25)
    w_short = bell_draw(keys[4], (CIN, COUT), CIN ** -0.5, 0.1875)
    w_branch = bell_draw(keys[5], (COUT, BR), COUT ** -0.5, 0.125)
    w_dilated = bell_draw(keys[6], (9, BR, BR), (9 * BR) ** -0.5, 0.125)
    return {"features": features, "assignment": assignment, "w_reduce": w_reduce, "w_expand": w_expand, "w_short": w_short, "w_branch": w_branch, "w_dilated": w_dilated}


def trunk(rows_in, w_reduce, w_expand, w_short, w_branch):
    hidden = jax.nn.relu(jnp.dot(rows_in, w_reduce, preferred_element_type=jnp.float32)).astype(jnp.bfloat16)
    summed = jnp.dot(hidden, w_expand, preferred_element_type=jnp.float32) + jnp.dot(rows_in, w_short, preferred_element_type=jnp.float32)
    block_out = jax.nn.relu(summed).astype(jnp.bfloat16)
    return jax.nn.relu(jnp.dot(block_out, w_branch, preferred_element_type=jnp.float32)).astype(jnp.bfloat16)


def reference(features, assignment, w_reduce, w_expand, w_short, w_branch, w_dilated):
    pixels = TILE * TILE
    tissue_count = N_ROW * N_COL * LOAD
    flat_in = features.reshape(TR * TC, pixels, CIN)
    tissue = assignment.reshape(TR * TC) >= 0
    chosen = jnp.nonzero(tissue, size=tissue_count)[0].astype(jnp.int32)
    picked = flat_in[chosen].reshape(tissue_count // LOAD, LOAD * pixels, CIN)

    def one_block(rows_in):
        return trunk(rows_in, w_reduce, w_expand, w_short, w_branch)

    reduced = lax.map(one_block, picked).reshape(tissue_count, pixels, BR)
    tile_grid = jnp.zeros((TR * TC, pixels, BR), jnp.bfloat16).at[chosen].set(reduced)
    height = TR * TILE
    width = TC * TILE
    feature_grid = tile_grid.reshape(TR, TC, TILE, TILE, BR).transpose(0, 2, 1, 3, 4).reshape(height, width, BR)
    padded = jnp.pad(feature_grid, ((RR, RR), (RC, RC), (0, 0)))
    summed = jnp.zeros((height * width, BR), jnp.float32)
    for down_tap in range(3):
        for side_tap in range(3):
            window = padded[down_tap * RR:down_tap * RR + height, side_tap * RC:side_tap * RC + width]
            summed = summed + jnp.dot(window.reshape(height * width, BR), w_dilated[3 * down_tap + side_tap], preferred_element_type=jnp.float32)
    return jax.nn.relu(summed).astype(jnp.bfloat16).reshape(height, width, BR)
```

```python
import functools

import jax
import jax.numpy as jnp
from jax import lax
from jax.experimental import pallas as pl
from jax.experimental.pallas import tpu as pltpu
from jax.sharding import PartitionSpec as P

TILE = 16
RR = 18
RC = 15
MESH = pl.DeviceIdType.MESH


def kernel(
    row_count, col_count,
    codes, features, w_reduce, w_expand, w_short, w_branch, w_dilated, out,
    xh, v_reduce, v_cat, v_branch, v_dilated, block, grid, stacked, acc, out_buf,
    x_sem, w_sem, out_sem, row_send, row_recv, col_send, col_recv,
):
    tile_rows, tile_cols, pixels, channels = features.shape
    mid = w_reduce.shape[1]
    cout = w_expand.shape[1]
    width = w_branch.shape[1]
    height = tile_rows * TILE
    row = lax.axis_index("row")
    col = lax.axis_index("col")
    has_up = row > 0
    has_down = row < row_count - 1
    has_left = col > 0
    has_right = col < col_count - 1
    sides = ((has_up, {"row": row - 1}), (has_down, {"row": row + 1}),
             (has_left, {"col": col - 1}), (has_right, {"col": col + 1}))

    def tile_col(step):
        return jnp.where(col == 0, tile_cols - 1 - step, step)

    def x_copy(tile_row, step):
        return pltpu.make_async_copy(
            features.at[tile_row, tile_col(step)],
            xh.at[tile_row, step, :, pl.ds(0, channels)],
            x_sem.at[tile_row, step],
        )

    last = tile_rows - 1
    reduce_copy = pltpu.make_async_copy(w_reduce, v_reduce, w_sem.at[0])
    short_copy = pltpu.make_async_copy(w_short, v_cat.at[pl.ds(0, channels)], w_sem.at[1])
    expand_copy = pltpu.make_async_copy(w_expand, v_cat.at[pl.ds(channels, mid)], w_sem.at[2])
    branch_copy = pltpu.make_async_copy(w_branch, v_branch, w_sem.at[3])
    dilated_copy = pltpu.make_async_copy(w_dilated, v_dilated, w_sem.at[4])
    x_copy(last, 0).start()
    reduce_copy.start()
    short_copy.start()
    expand_copy.start()
    branch_copy.start()
    for tile_row in reversed(range(last)):
        x_copy(tile_row, 0).start()
    for step in range(1, tile_cols):
        for tile_row in reversed(range(tile_rows)):
            x_copy(tile_row, step).start()
    dilated_copy.start()

    barrier = pltpu.get_barrier_semaphore()
    for there, device in sides:
        @pl.when(there)
        def _(device=device):
            pl.semaphore_signal(barrier, inc=1, device_id=device, device_id_type=MESH)

    @pl.when(jnp.logical_not(has_up))
    def _():
        grid[0:RR] = jnp.zeros((RR,) + grid.shape[1:], grid.dtype)

    @pl.when(jnp.logical_not(has_down))
    def _():
        grid[RR + height:] = jnp.zeros((RR,) + grid.shape[1:], grid.dtype)

    @pl.when(jnp.logical_not(has_left))
    def _():
        grid[:, 0] = jnp.zeros((grid.shape[0],) + grid.shape[2:], grid.dtype)

    @pl.when(jnp.logical_not(has_right))
    def _():
        grid[:, tile_cols + 1] = jnp.zeros((grid.shape[0],) + grid.shape[2:], grid.dtype)

    strip = RR - TILE

    def row_copy(kind, step):
        at = tile_col(step) + 1
        if kind == 0:
            src, dst, size, device = height + RR - TILE, strip, TILE, {"row": row + 1}
        elif kind == 1:
            src, dst, size, device = height, 0, strip, {"row": row + 1}
        else:
            src, dst, size, device = RR, RR + height, RR, {"row": row - 1}
        return pltpu.make_async_remote_copy(
            src_ref=grid.at[pl.ds(src, size), at],
            dst_ref=grid.at[pl.ds(dst, size), at],
            send_sem=row_send.at[kind, step],
            recv_sem=row_recv.at[kind, step],
            device_id=device,
            device_id_type=MESH,
        )

    def col_copy(side, part):
        start, size = ((RR, height), (0, RR), (RR + height, RR))[part]
        if side == 0:
            src, dst, device = 1, tile_cols + 1, {"col": col - 1}
        else:
            src, dst, device = tile_cols, 0, {"col": col + 1}
        return pltpu.make_async_remote_copy(
            src_ref=grid.at[pl.ds(start, size), src],
            dst_ref=grid.at[pl.ds(start, size), dst],
            send_sem=col_send.at[side, part],
            recv_sem=col_recv.at[side, part],
            device_id=device,
            device_id_type=MESH,
        )

    def send_col(step, part):
        at = tile_col(step)

        @pl.when(jnp.logical_and(has_left, at == 0))
        def _():
            col_copy(0, part).start()

        @pl.when(jnp.logical_and(has_right, at == tile_cols - 1))
        def _():
            col_copy(1, part).start()

    @pl.loop(0, tile_cols)
    def _(step):
        for tile_row in reversed(range(tile_rows)):
            x_copy(tile_row, step).wait()
            first = jnp.logical_and(step == 0, tile_row == last)
            if tile_row == last:
                pl.when(step == 0)(reduce_copy.wait)
            x = xh.at[tile_row, step]
            hidden = jnp.dot(x[:, 0:channels], v_reduce[...], preferred_element_type=jnp.float32)
            x[:, channels:channels + mid] = jnp.maximum(hidden, 0.0).astype(jnp.bfloat16)
            if tile_row == last:
                @pl.when(step == 0)
                def _():
                    short_copy.wait()
                    expand_copy.wait()
            piece = 512
            for start in range(0, cout, piece):
                summed = jnp.dot(
                    x[...], v_cat[:, start:start + piece], preferred_element_type=jnp.float32
                )
                block[:, start:start + piece] = jnp.maximum(summed, 0.0).astype(jnp.bfloat16)
            if tile_row == last:
                pl.when(step == 0)(branch_copy.wait)
            reduced = jnp.dot(block[...], v_branch[...], preferred_element_type=jnp.float32)
            at = tile_col(step)
            kept = (codes[tile_row, at] >= 0).astype(jnp.float32)
            reduced = (jnp.maximum(reduced, 0.0) * kept).astype(jnp.bfloat16)
            grid[pl.ds(RR + tile_row * TILE, TILE), at + 1] = reduced.reshape(TILE, TILE, width)
            if tile_row == last:
                @pl.when(step == 0)
                def _():
                    total = (has_up.astype(jnp.int32) + has_down.astype(jnp.int32)
                             + has_left.astype(jnp.int32) + has_right.astype(jnp.int32))
                    pl.semaphore_wait(barrier, total)

                @pl.when(has_down)
                def _():
                    row_copy(0, step).start()

        @pl.when(has_down)
        def _():
            row_copy(1, step).start()

        @pl.when(has_up)
        def _():
            row_copy(2, step).start()

        send_col(step, 0)

    def wait_rows(step):
        @pl.when(has_up)
        def _():
            row_copy(0, step).wait_recv()
            row_copy(1, step).wait_recv()

        @pl.when(has_down)
        def _():
            row_copy(2, step).wait_recv()

    def forward(step):
        pl.when(has_up)(functools.partial(send_col, step, 1))
        pl.when(has_down)(functools.partial(send_col, step, 2))

    def wait_col(part):
        @pl.when(has_right)
        def _():
            col_copy(0, part).wait_recv()

        @pl.when(has_left)
        def _():
            col_copy(1, part).wait_recv()

    span = (tile_cols + 2) * TILE
    out_width = tile_cols * TILE

    def stack(start, count, group):
        @pl.loop(0, count // group)
        def _(index):
            first_row = start + index * group
            rows = grid[pl.ds(first_row, group)].reshape(group * span, width)
            wide = rows.astype(jnp.float32)
            size = group * span
            shift = TILE - RC
            before = pltpu.roll(wide, size - shift, 0).astype(jnp.bfloat16)
            after = pltpu.roll(wide, shift, 0).astype(jnp.bfloat16)
            here = pl.ds(first_row, group)
            stacked[here, :, 0:width] = before.reshape(group, span, width)[:, 0:out_width]
            stacked[here, :, width:2 * width] = rows.reshape(group, span, width)[:, TILE:TILE + out_width]
            stacked[here, :, 2 * width:] = after.reshape(group, span, width)[:, 2 * TILE:]

    def tap(first_row, count, down_tap):
        rows = stacked[pl.ds(first_row, count)].reshape(count * out_width, 3 * width)
        weights = v_dilated[3 * down_tap:3 * down_tap + 3].reshape(3 * width, width)
        return jnp.dot(rows, weights, preferred_element_type=jnp.float32).reshape(
            count, out_width, width
        )

    wait_rows(0)
    forward(0)
    wait_col(0)
    dilated_copy.wait()
    stack(RR, height, 2)
    inner = height - RR

    @pl.loop(0, 4)
    def _(index):
        size = height // 4
        acc[pl.ds(index * size, size)] = tap(RR + index * size, size, 1)

    @pl.loop(0, 2)
    def _(index):
        size = inner // 2
        acc[pl.ds(RR + index * size, size)] += tap(RR + index * size, size, 0)
        acc[pl.ds(index * size, size)] += tap(2 * RR + index * size, size, 2)

    for step in range(1, tile_cols):
        wait_rows(step)
        forward(step)
    pl.when(has_up)(functools.partial(wait_col, 1))
    pl.when(has_down)(functools.partial(wait_col, 2))

    def finish(start, size, taps):
        total = acc[pl.ds(start, size)]
        for down_tap in taps:
            total = total + tap(start + RR * down_tap, size, down_tap)
        out_buf[pl.ds(start, size)] = jnp.maximum(total, 0.0).astype(jnp.bfloat16)

    stack(0, RR, 2)

    @pl.loop(0, 2)
    def _(index):
        finish(index * (inner // 2), inner // 2, (0,))

    upper = pltpu.make_async_copy(out_buf.at[pl.ds(0, inner)], out.at[pl.ds(0, inner)], out_sem.at[0])
    upper.start()
    stack(RR + height, RR, 2)
    finish(inner, RR - inner, (0, 2))

    @pl.loop(0, 2)
    def _(index):
        finish(RR + index * (inner // 2), inner // 2, (2,))

    lower = pltpu.make_async_copy(out_buf.at[pl.ds(inner, RR)], out.at[pl.ds(inner, RR)], out_sem.at[1])
    lower.start()

    for step in range(tile_cols):
        @pl.when(has_down)
        def _(step=step):
            row_copy(0, step).wait_send()
            row_copy(1, step).wait_send()

        @pl.when(has_up)
        def _(step=step):
            row_copy(2, step).wait_send()

    for side, there in ((0, has_left), (1, has_right)):
        for part, other in ((0, None), (1, has_up), (2, has_down)):
            ready = there if other is None else jnp.logical_and(there, other)
            pl.when(ready)(col_copy(side, part).wait_send)
    upper.wait()
    lower.wait()


def shards(row_count, col_count, features, assignment, w_reduce, w_expand, w_short, w_branch, w_dilated):
    tile_rows, tile_cols, pixels, channels = features.shape
    mid = w_reduce.shape[1]
    cout = w_expand.shape[1]
    width = w_branch.shape[1]
    height = tile_rows * TILE
    out_width = tile_cols * TILE
    bf16 = jnp.bfloat16
    any_spec = pl.BlockSpec(memory_space=pl.ANY)
    per_pixel = channels * mid + (channels + mid) * cout + cout * width + 9 * width * width
    return pl.pallas_call(
        functools.partial(kernel, row_count, col_count),
        out_shape=jax.ShapeDtypeStruct((height, out_width, width), bf16),
        in_specs=[pl.BlockSpec(memory_space=pltpu.SMEM)] + [any_spec] * 6,
        out_specs=any_spec,
        scratch_shapes=[
            pltpu.VMEM((tile_rows, tile_cols, pixels, channels + mid), bf16),
            pltpu.VMEM((channels, mid), bf16),
            pltpu.VMEM((channels + mid, cout), bf16),
            pltpu.VMEM((cout, width), bf16),
            pltpu.VMEM(w_dilated.shape, bf16),
            pltpu.VMEM((pixels, cout), bf16),
            pltpu.VMEM((height + 2 * RR, tile_cols + 2, TILE, width), bf16),
            pltpu.VMEM((height + 2 * RR, out_width, 3 * width), bf16),
            pltpu.VMEM((height, out_width, width), jnp.float32),
            pltpu.VMEM((height, out_width, width), bf16),
            pltpu.SemaphoreType.DMA((tile_rows, tile_cols)),
            pltpu.SemaphoreType.DMA((5,)),
            pltpu.SemaphoreType.DMA((2,)),
            pltpu.SemaphoreType.DMA((3, tile_cols)),
            pltpu.SemaphoreType.DMA((3, tile_cols)),
            pltpu.SemaphoreType.DMA((2, 3)),
            pltpu.SemaphoreType.DMA((2, 3)),
        ],
        cost_estimate=pl.CostEstimate(
            flops=2 * height * out_width * per_pixel, bytes_accessed=15 * 2 ** 20, transcendentals=0
        ),
        compiler_params=pltpu.CompilerParams(
            collective_id=0, has_side_effects=True, vmem_limit_bytes=56 * 2 ** 20
        ),
    )(assignment, features, w_reduce, w_expand, w_short, w_branch, w_dilated)


def solution(mesh):
    in_specs = (
        P(("groups", "row"), "col", None, None),
        P(("groups", "row"), "col"),
        P(),
        P(),
        P(),
        P(),
        P(),
    )
    out_specs = P(("groups", "row"), "col", None)
    return jax.shard_map(
        functools.partial(shards, mesh.shape["row"], mesh.shape["col"]),
        mesh=mesh, in_specs=in_specs, out_specs=out_specs, check_vma=False,
    )
```

```python
import functools

import jax
import jax.numpy as jnp
from jax import lax
from jax.experimental import pallas as pl
from jax.experimental.pallas import tpu as pltpu
from jax.sharding import PartitionSpec as P

TILE = 16
RR = 18
RC = 15
PIECE = 512
MESH = pl.DeviceIdType.MESH


def kernel(
    row_count, col_count,
    codes, features, w_reduce, w_expand, w_short, w_branch, w_dilated, out,
    xh, v_reduce, v_cat, v_branch, v_dilated, block, grid, stacked, acc, out_buf,
    x_sem, w_sem, cat_sem, out_sem, row_send, row_recv, col_send, col_recv,
):
    tile_rows, tile_cols, pixels, channels = features.shape
    mid = w_reduce.shape[1]
    cout = w_expand.shape[1]
    width = w_branch.shape[1]
    height = tile_rows * TILE
    row = lax.axis_index("row")
    col = lax.axis_index("col")
    has_up = row > 0
    has_down = row < row_count - 1
    has_left = col > 0
    has_right = col < col_count - 1
    sides = ((has_up, {"row": row - 1}), (has_down, {"row": row + 1}),
             (has_left, {"col": col - 1}), (has_right, {"col": col + 1}))

    def tile_col(step):
        return jnp.where(col == 0, tile_cols - 1 - step, step)

    def x_copy(tile_row, step):
        return pltpu.make_async_copy(
            features.at[tile_row, tile_col(step)],
            xh.at[tile_row, step, :, pl.ds(0, channels)],
            x_sem.at[tile_row, step],
        )

    last = tile_rows - 1
    reduce_copy = pltpu.make_async_copy(w_reduce, v_reduce, w_sem.at[0])

    def cat_copies(piece):
        columns = pl.ds(piece * PIECE, PIECE)
        return [
            pltpu.make_async_copy(
                part.at[:, columns], v_cat.at[pl.ds(first, part.shape[0]), columns], cat_sem.at[at, piece]
            )
            for at, (part, first) in enumerate(((w_short, 0), (w_expand, channels)))
        ]

    branch_copy = pltpu.make_async_copy(w_branch, v_branch, w_sem.at[1])
    dilated_copy = pltpu.make_async_copy(w_dilated, v_dilated, w_sem.at[2])
    x_copy(last, 0).start()
    reduce_copy.start()
    for piece in range(cout // PIECE):
        for copy in cat_copies(piece):
            copy.start()
    branch_copy.start()

    barrier = pltpu.get_barrier_semaphore()
    for there, device in sides:
        @pl.when(there)
        def _(device=device):
            pl.semaphore_signal(barrier, inc=1, device_id=device, device_id_type=MESH)

    @pl.when(jnp.logical_not(has_up))
    def _():
        grid[0:RR] = jnp.zeros((RR,) + grid.shape[1:], grid.dtype)

    @pl.when(jnp.logical_not(has_down))
    def _():
        grid[RR + height:] = jnp.zeros((RR,) + grid.shape[1:], grid.dtype)

    @pl.when(jnp.logical_not(has_left))
    def _():
        grid[:, 0] = jnp.zeros((grid.shape[0],) + grid.shape[2:], grid.dtype)

    @pl.when(jnp.logical_not(has_right))
    def _():
        grid[:, tile_cols + 1] = jnp.zeros((grid.shape[0],) + grid.shape[2:], grid.dtype)

    strip = RR - TILE

    def row_copy(kind, step):
        at = tile_col(step) + 1
        if kind == 0:
            src, dst, size, device = height + RR - TILE, strip, TILE, {"row": row + 1}
        elif kind == 1:
            src, dst, size, device = height, 0, strip, {"row": row + 1}
        else:
            src, dst, size, device = RR, RR + height, RR, {"row": row - 1}
        return pltpu.make_async_remote_copy(
            src_ref=grid.at[pl.ds(src, size), at],
            dst_ref=grid.at[pl.ds(dst, size), at],
            send_sem=row_send.at[kind, step],
            recv_sem=row_recv.at[kind, step],
            device_id=device,
            device_id_type=MESH,
        )

    def col_copy(side, part):
        start, size = ((RR, height), (0, RR), (RR + height, RR))[part]
        if side == 0:
            src, dst, device = 1, tile_cols + 1, {"col": col - 1}
        else:
            src, dst, device = tile_cols, 0, {"col": col + 1}
        return pltpu.make_async_remote_copy(
            src_ref=grid.at[pl.ds(start, size), src],
            dst_ref=grid.at[pl.ds(start, size), dst],
            send_sem=col_send.at[side, part],
            recv_sem=col_recv.at[side, part],
            device_id=device,
            device_id_type=MESH,
        )

    def send_col(step, part):
        at = tile_col(step)

        @pl.when(jnp.logical_and(has_left, at == 0))
        def _():
            col_copy(0, part).start()

        @pl.when(jnp.logical_and(has_right, at == tile_cols - 1))
        def _():
            col_copy(1, part).start()

    @pl.loop(0, tile_cols)
    def _(step):
        for tile_row in reversed(range(tile_rows)):
            x_copy(tile_row, step).wait()
            if tile_row == last:
                pl.when(step == 0)(reduce_copy.wait)
            x = xh.at[tile_row, step]
            hidden = jnp.dot(x[:, 0:channels], v_reduce[...], preferred_element_type=jnp.float32)
            x[:, channels:channels + mid] = jnp.maximum(hidden, 0.0).astype(jnp.bfloat16)
            for piece in range(cout // PIECE):
                if tile_row == last:
                    @pl.when(step == 0)
                    def _(piece=piece):
                        for copy in cat_copies(piece):
                            copy.wait()
                columns = slice(piece * PIECE, (piece + 1) * PIECE)
                summed = jnp.dot(x[...], v_cat[:, columns], preferred_element_type=jnp.float32)
                block[:, columns] = jnp.maximum(summed, 0.0).astype(jnp.bfloat16)
            if tile_row == last:
                @pl.when(step == 0)
                def _():
                    branch_copy.wait()
                    for other in reversed(range(last)):
                        x_copy(other, 0).start()
                    dilated_copy.start()

                @pl.when(step < tile_cols - 1)
                def _():
                    for other in reversed(range(tile_rows)):
                        x_copy(other, step + 1).start()
            reduced = jnp.dot(block[...], v_branch[...], preferred_element_type=jnp.float32)
            at = tile_col(step)
            kept = (codes[tile_row, at] >= 0).astype(jnp.float32)
            reduced = (jnp.maximum(reduced, 0.0) * kept).astype(jnp.bfloat16)
            grid[pl.ds(RR + tile_row * TILE, TILE), at + 1] = reduced.reshape(TILE, TILE, width)
            if tile_row == last:
                @pl.when(step == 0)
                def _():
                    total = (has_up.astype(jnp.int32) + has_down.astype(jnp.int32)
                             + has_left.astype(jnp.int32) + has_right.astype(jnp.int32))
                    pl.semaphore_wait(barrier, total)

                @pl.when(has_down)
                def _():
                    row_copy(0, step).start()

        @pl.when(has_down)
        def _():
            row_copy(1, step).start()

        @pl.when(has_up)
        def _():
            row_copy(2, step).start()

        send_col(step, 0)

    def wait_rows(step):
        @pl.when(has_up)
        def _():
            row_copy(0, step).wait_recv()
            row_copy(1, step).wait_recv()

        @pl.when(has_down)
        def _():
            row_copy(2, step).wait_recv()

    def forward(step):
        pl.when(has_up)(functools.partial(send_col, step, 1))
        pl.when(has_down)(functools.partial(send_col, step, 2))

    def wait_col(part):
        @pl.when(has_right)
        def _():
            col_copy(0, part).wait_recv()

        @pl.when(has_left)
        def _():
            col_copy(1, part).wait_recv()

    span = (tile_cols + 2) * TILE
    out_width = tile_cols * TILE

    def stack(start, count, group):
        @pl.loop(0, count // group)
        def _(index):
            first_row = start + index * group
            rows = grid[pl.ds(first_row, group)].reshape(group * span, width)
            wide = rows.astype(jnp.float32)
            size = group * span
            shift = TILE - RC
            before = pltpu.roll(wide, size - shift, 0).astype(jnp.bfloat16)
            after = pltpu.roll(wide, shift, 0).astype(jnp.bfloat16)
            here = pl.ds(first_row, group)
            stacked[here, :, 0:width] = before.reshape(group, span, width)[:, 0:out_width]
            stacked[here, :, width:2 * width] = rows.reshape(group, span, width)[:, TILE:TILE + out_width]
            stacked[here, :, 2 * width:] = after.reshape(group, span, width)[:, 2 * TILE:]

    def tap(first_row, count, down_tap):
        rows = stacked[pl.ds(first_row, count)].reshape(count * out_width, 3 * width)
        weights = v_dilated[3 * down_tap:3 * down_tap + 3].reshape(3 * width, width)
        return jnp.dot(rows, weights, preferred_element_type=jnp.float32).reshape(
            count, out_width, width
        )

    wait_rows(0)
    forward(0)
    wait_col(0)
    dilated_copy.wait()
    stack(RR, height, 2)
    inner = height - RR

    @pl.loop(0, 4)
    def _(index):
        size = height // 4
        acc[pl.ds(index * size, size)] = tap(RR + index * size, size, 1)

    @pl.loop(0, 2)
    def _(index):
        size = inner // 2
        acc[pl.ds(RR + index * size, size)] += tap(RR + index * size, size, 0)
        acc[pl.ds(index * size, size)] += tap(2 * RR + index * size, size, 2)

    for step in range(1, tile_cols):
        wait_rows(step)
        forward(step)
    pl.when(has_up)(functools.partial(wait_col, 1))
    pl.when(has_down)(functools.partial(wait_col, 2))

    def finish(start, size, taps):
        total = acc[pl.ds(start, size)]
        for down_tap in taps:
            total = total + tap(start + RR * down_tap, size, down_tap)
        out_buf[pl.ds(start, size)] = total.astype(jnp.bfloat16)

    stack(0, RR, 2)

    @pl.loop(0, 2)
    def _(index):
        finish(index * (inner // 2), inner // 2, (0,))

    upper = pltpu.make_async_copy(out_buf.at[pl.ds(0, inner)], out.at[pl.ds(0, inner)], out_sem.at[0])
    upper.start()
    stack(RR + height, RR, 2)
    finish(inner, RR - inner, (0, 2))

    @pl.loop(0, 2)
    def _(index):
        finish(RR + index * (inner // 2), inner // 2, (2,))

    lower = pltpu.make_async_copy(out_buf.at[pl.ds(inner, RR)], out.at[pl.ds(inner, RR)], out_sem.at[1])
    lower.start()

    for step in range(tile_cols):
        @pl.when(has_down)
        def _(step=step):
            row_copy(0, step).wait_send()
            row_copy(1, step).wait_send()

        @pl.when(has_up)
        def _(step=step):
            row_copy(2, step).wait_send()

    for side, there in ((0, has_left), (1, has_right)):
        for part, other in ((0, None), (1, has_up), (2, has_down)):
            ready = there if other is None else jnp.logical_and(there, other)
            pl.when(ready)(col_copy(side, part).wait_send)
    upper.wait()
    lower.wait()


def shards(row_count, col_count, features, assignment, w_reduce, w_expand, w_short, w_branch, w_dilated):
    tile_rows, tile_cols, pixels, channels = features.shape
    mid = w_reduce.shape[1]
    cout = w_expand.shape[1]
    width = w_branch.shape[1]
    height = tile_rows * TILE
    out_width = tile_cols * TILE
    bf16 = jnp.bfloat16
    any_spec = pl.BlockSpec(memory_space=pl.ANY)
    per_pixel = channels * mid + (channels + mid) * cout + cout * width + 9 * width * width
    summed = pl.pallas_call(
        functools.partial(kernel, row_count, col_count),
        out_shape=jax.ShapeDtypeStruct((height, out_width, width), bf16),
        in_specs=[pl.BlockSpec(memory_space=pltpu.SMEM)] + [any_spec] * 6,
        out_specs=any_spec,
        scratch_shapes=[
            pltpu.VMEM((tile_rows, tile_cols, pixels, channels + mid), bf16),
            pltpu.VMEM((channels, mid), bf16),
            pltpu.VMEM((channels + mid, cout), bf16),
            pltpu.VMEM((cout, width), bf16),
            pltpu.VMEM(w_dilated.shape, bf16),
            pltpu.VMEM((pixels, cout), bf16),
            pltpu.VMEM((height + 2 * RR, tile_cols + 2, TILE, width), bf16),
            pltpu.VMEM((height + 2 * RR, out_width, 3 * width), bf16),
            pltpu.VMEM((height, out_width, width), jnp.float32),
            pltpu.VMEM((height, out_width, width), bf16),
            pltpu.SemaphoreType.DMA((tile_rows, tile_cols)),
            pltpu.SemaphoreType.DMA((3,)),
            pltpu.SemaphoreType.DMA((2, cout // PIECE)),
            pltpu.SemaphoreType.DMA((2,)),
            pltpu.SemaphoreType.DMA((3, tile_cols)),
            pltpu.SemaphoreType.DMA((3, tile_cols)),
            pltpu.SemaphoreType.DMA((2, 3)),
            pltpu.SemaphoreType.DMA((2, 3)),
        ],
        cost_estimate=pl.CostEstimate(
            flops=2 * height * out_width * per_pixel, bytes_accessed=15 * 2 ** 20, transcendentals=0
        ),
        compiler_params=pltpu.CompilerParams(
            collective_id=0, has_side_effects=True, vmem_limit_bytes=52 * 2 ** 20
        ),
    )(assignment, features, w_reduce, w_expand, w_short, w_branch, w_dilated)
    return jnp.maximum(summed, jnp.zeros((), bf16))


def solution(mesh):
    in_specs = (
        P(("groups", "row"), "col", None, None),
        P(("groups", "row"), "col"),
        P(),
        P(),
        P(),
        P(),
        P(),
    )
    out_specs = P(("groups", "row"), "col", None)
    return jax.shard_map(
        functools.partial(shards, mesh.shape["row"], mesh.shape["col"]),
        mesh=mesh, in_specs=in_specs, out_specs=out_specs, check_vma=False,
    )
```

```python
import functools

import jax
import jax.numpy as jnp
from jax import lax
from jax.experimental import pallas as pl
from jax.experimental.pallas import tpu as pltpu
from jax.sharding import PartitionSpec as P

TILE = 16
RR = 18
RC = 15
MESH = pl.DeviceIdType.MESH


def kernel(
    row_count, col_count,
    codes, features, w_reduce, w_expand, w_short, w_branch, w_dilated, out,
    xh, v_reduce, v_cat, v_branch, v_dilated, block, grid, stacked, acc, out_buf,
    x_sem, w_sem, out_sem, row_send, row_recv, col_send, col_recv,
):
    tile_rows, tile_cols, pixels, channels = features.shape
    mid = w_reduce.shape[1]
    cout = w_expand.shape[1]
    width = w_branch.shape[1]
    height = tile_rows * TILE
    row = lax.axis_index("row")
    col = lax.axis_index("col")
    has_up = row > 0
    has_down = row < row_count - 1
    has_left = col > 0
    has_right = col < col_count - 1
    sides = ((has_up, {"row": row - 1}), (has_down, {"row": row + 1}),
             (has_left, {"col": col - 1}), (has_right, {"col": col + 1}))

    def tile_col(step):
        return jnp.where(col == 0, tile_cols - 1 - step, step)

    def x_copy(tile_row, step):
        return pltpu.make_async_copy(
            features.at[tile_row, tile_col(step)],
            xh.at[tile_row, step, :, pl.ds(0, channels)],
            x_sem.at[tile_row, step],
        )

    last = tile_rows - 1
    reduce_copy = pltpu.make_async_copy(w_reduce, v_reduce, w_sem.at[0])
    short_copy = pltpu.make_async_copy(w_short, v_cat.at[pl.ds(0, channels)], w_sem.at[1])
    expand_copy = pltpu.make_async_copy(w_expand, v_cat.at[pl.ds(channels, mid)], w_sem.at[2])
    branch_copy = pltpu.make_async_copy(w_branch, v_branch, w_sem.at[3])
    dilated_copy = pltpu.make_async_copy(w_dilated, v_dilated, w_sem.at[4])
    x_copy(last, 0).start()
    reduce_copy.start()
    short_copy.start()
    expand_copy.start()
    branch_copy.start()
    for tile_row in reversed(range(last)):
        x_copy(tile_row, 0).start()
    for step in range(1, tile_cols):
        for tile_row in reversed(range(tile_rows)):
            x_copy(tile_row, step).start()
    dilated_copy.start()

    barrier = pltpu.get_barrier_semaphore()
    for there, device in sides:
        @pl.when(there)
        def _(device=device):
            pl.semaphore_signal(barrier, inc=1, device_id=device, device_id_type=MESH)

    @pl.when(jnp.logical_not(has_up))
    def _():
        grid[0:RR] = jnp.zeros((RR,) + grid.shape[1:], grid.dtype)

    @pl.when(jnp.logical_not(has_down))
    def _():
        grid[RR + height:] = jnp.zeros((RR,) + grid.shape[1:], grid.dtype)

    @pl.when(jnp.logical_not(has_left))
    def _():
        grid[:, 0] = jnp.zeros((grid.shape[0],) + grid.shape[2:], grid.dtype)

    @pl.when(jnp.logical_not(has_right))
    def _():
        grid[:, tile_cols + 1] = jnp.zeros((grid.shape[0],) + grid.shape[2:], grid.dtype)

    strip = RR - TILE

    def row_copy(kind, step):
        at = tile_col(step) + 1
        if kind == 0:
            src, dst, size, device = height + RR - TILE, strip, TILE, {"row": row + 1}
        elif kind == 1:
            src, dst, size, device = height, 0, strip, {"row": row + 1}
        else:
            src, dst, size, device = RR, RR + height, RR, {"row": row - 1}
        return pltpu.make_async_remote_copy(
            src_ref=grid.at[pl.ds(src, size), at],
            dst_ref=grid.at[pl.ds(dst, size), at],
            send_sem=row_send.at[kind, step],
            recv_sem=row_recv.at[kind, step],
            device_id=device,
            device_id_type=MESH,
        )

    def col_copy(side, part):
        start, size = ((RR, height), (0, RR), (RR + height, RR))[part]
        if side == 0:
            src, dst, device = 1, tile_cols + 1, {"col": col - 1}
        else:
            src, dst, device = tile_cols, 0, {"col": col + 1}
        return pltpu.make_async_remote_copy(
            src_ref=grid.at[pl.ds(start, size), src],
            dst_ref=grid.at[pl.ds(start, size), dst],
            send_sem=col_send.at[side, part],
            recv_sem=col_recv.at[side, part],
            device_id=device,
            device_id_type=MESH,
        )

    def send_col(step, part):
        at = tile_col(step)

        @pl.when(jnp.logical_and(has_left, at == 0))
        def _():
            col_copy(0, part).start()

        @pl.when(jnp.logical_and(has_right, at == tile_cols - 1))
        def _():
            col_copy(1, part).start()

    @pl.loop(0, tile_cols)
    def _(step):
        for tile_row in reversed(range(tile_rows)):
            x_copy(tile_row, step).wait()
            first = jnp.logical_and(step == 0, tile_row == last)
            if tile_row == last:
                pl.when(step == 0)(reduce_copy.wait)
            x = xh.at[tile_row, step]
            hidden = jnp.dot(x[:, 0:channels], v_reduce[...], preferred_element_type=jnp.float32)
            x[:, channels:channels + mid] = jnp.maximum(hidden, 0.0).astype(jnp.bfloat16)
            if tile_row == last:
                @pl.when(step == 0)
                def _():
                    short_copy.wait()
                    expand_copy.wait()
            piece = 512
            for start in range(0, cout, piece):
                summed = jnp.dot(
                    x[...], v_cat[:, start:start + piece], preferred_element_type=jnp.float32
                )
                block[:, start:start + piece] = jnp.maximum(summed, 0.0).astype(jnp.bfloat16)
            if tile_row == last:
                pl.when(step == 0)(branch_copy.wait)
            reduced = jnp.dot(block[...], v_branch[...], preferred_element_type=jnp.float32)
            at = tile_col(step)
            kept = (codes[tile_row, at] >= 0).astype(jnp.float32)
            reduced = (jnp.maximum(reduced, 0.0) * kept).astype(jnp.bfloat16)
            grid[pl.ds(RR + tile_row * TILE, TILE), at + 1] = reduced.reshape(TILE, TILE, width)
            if tile_row == last:
                @pl.when(step == 0)
                def _():
                    total = (has_up.astype(jnp.int32) + has_down.astype(jnp.int32)
                             + has_left.astype(jnp.int32) + has_right.astype(jnp.int32))
                    pl.semaphore_wait(barrier, total)

                @pl.when(has_down)
                def _():
                    row_copy(0, step).start()

        @pl.when(has_down)
        def _():
            row_copy(1, step).start()

        @pl.when(has_up)
        def _():
            row_copy(2, step).start()

        send_col(step, 0)

    def wait_above(step):
        @pl.when(has_up)
        def _():
            row_copy(0, step).wait_recv()
            row_copy(1, step).wait_recv()
            send_col(step, 1)

    def wait_below(step):
        @pl.when(has_down)
        def _():
            row_copy(2, step).wait_recv()
            send_col(step, 2)

    def wait_col(part):
        @pl.when(has_right)
        def _():
            col_copy(0, part).wait_recv()

        @pl.when(has_left)
        def _():
            col_copy(1, part).wait_recv()

    span = (tile_cols + 2) * TILE
    out_width = tile_cols * TILE

    def stack(start, count, group):
        @pl.loop(0, count // group)
        def _(index):
            first_row = start + index * group
            rows = grid[pl.ds(first_row, group)].reshape(group * span, width)
            wide = rows.astype(jnp.float32)
            size = group * span
            shift = TILE - RC
            before = pltpu.roll(wide, size - shift, 0).astype(jnp.bfloat16)
            after = pltpu.roll(wide, shift, 0).astype(jnp.bfloat16)
            here = pl.ds(first_row, group)
            stacked[here, :, 0:width] = before.reshape(group, span, width)[:, 0:out_width]
            stacked[here, :, width:2 * width] = rows.reshape(group, span, width)[:, TILE:TILE + out_width]
            stacked[here, :, 2 * width:] = after.reshape(group, span, width)[:, 2 * TILE:]

    def tap(first_row, count, down_tap):
        rows = stacked[pl.ds(first_row, count)].reshape(count * out_width, 3 * width)
        weights = v_dilated[3 * down_tap:3 * down_tap + 3].reshape(3 * width, width)
        return jnp.dot(rows, weights, preferred_element_type=jnp.float32).reshape(
            count, out_width, width
        )

    wait_above(0)
    wait_below(0)
    wait_col(0)
    dilated_copy.wait()
    stack(RR, height, 2)
    inner = height - RR

    @pl.loop(0, 4)
    def _(index):
        size = height // 4
        acc[pl.ds(index * size, size)] = tap(RR + index * size, size, 1)

    @pl.loop(0, 2)
    def _(index):
        size = inner // 2
        acc[pl.ds(RR + index * size, size)] += tap(RR + index * size, size, 0)
        acc[pl.ds(index * size, size)] += tap(2 * RR + index * size, size, 2)

    for step in range(1, tile_cols):
        wait_above(step)
    pl.when(has_up)(functools.partial(wait_col, 1))

    def finish(start, size, taps):
        total = acc[pl.ds(start, size)]
        for down_tap in taps:
            total = total + tap(start + RR * down_tap, size, down_tap)
        out_buf[pl.ds(start, size)] = total.astype(jnp.bfloat16)

    stack(0, RR, 2)

    @pl.loop(0, 2)
    def _(index):
        finish(index * (inner // 2), inner // 2, (0,))

    upper = pltpu.make_async_copy(out_buf.at[pl.ds(0, inner)], out.at[pl.ds(0, inner)], out_sem.at[0])
    upper.start()
    for step in range(1, tile_cols):
        wait_below(step)
    pl.when(has_down)(functools.partial(wait_col, 2))
    stack(RR + height, RR, 2)
    finish(inner, RR - inner, (0, 2))

    @pl.loop(0, 2)
    def _(index):
        finish(RR + index * (inner // 2), inner // 2, (2,))

    lower = pltpu.make_async_copy(out_buf.at[pl.ds(inner, RR)], out.at[pl.ds(inner, RR)], out_sem.at[1])
    lower.start()

    for step in range(tile_cols):
        @pl.when(has_down)
        def _(step=step):
            row_copy(0, step).wait_send()
            row_copy(1, step).wait_send()

        @pl.when(has_up)
        def _(step=step):
            row_copy(2, step).wait_send()

    for side, there in ((0, has_left), (1, has_right)):
        for part, other in ((0, None), (1, has_up), (2, has_down)):
            ready = there if other is None else jnp.logical_and(there, other)
            pl.when(ready)(col_copy(side, part).wait_send)
    upper.wait()
    lower.wait()


def shards(row_count, col_count, features, assignment, w_reduce, w_expand, w_short, w_branch, w_dilated):
    tile_rows, tile_cols, pixels, channels = features.shape
    mid = w_reduce.shape[1]
    cout = w_expand.shape[1]
    width = w_branch.shape[1]
    height = tile_rows * TILE
    out_width = tile_cols * TILE
    bf16 = jnp.bfloat16
    any_spec = pl.BlockSpec(memory_space=pl.ANY)
    per_pixel = channels * mid + (channels + mid) * cout + cout * width + 9 * width * width
    summed = pl.pallas_call(
        functools.partial(kernel, row_count, col_count),
        out_shape=jax.ShapeDtypeStruct((height, out_width, width), bf16),
        in_specs=[pl.BlockSpec(memory_space=pltpu.SMEM)] + [any_spec] * 6,
        out_specs=any_spec,
        scratch_shapes=[
            pltpu.VMEM((tile_rows, tile_cols, pixels, channels + mid), bf16),
            pltpu.VMEM((channels, mid), bf16),
            pltpu.VMEM((channels + mid, cout), bf16),
            pltpu.VMEM((cout, width), bf16),
            pltpu.VMEM(w_dilated.shape, bf16),
            pltpu.VMEM((pixels, cout), bf16),
            pltpu.VMEM((height + 2 * RR, tile_cols + 2, TILE, width), bf16),
            pltpu.VMEM((height + 2 * RR, out_width, 3 * width), bf16),
            pltpu.VMEM((height, out_width, width), jnp.float32),
            pltpu.VMEM((height, out_width, width), bf16),
            pltpu.SemaphoreType.DMA((tile_rows, tile_cols)),
            pltpu.SemaphoreType.DMA((5,)),
            pltpu.SemaphoreType.DMA((2,)),
            pltpu.SemaphoreType.DMA((3, tile_cols)),
            pltpu.SemaphoreType.DMA((3, tile_cols)),
            pltpu.SemaphoreType.DMA((2, 3)),
            pltpu.SemaphoreType.DMA((2, 3)),
        ],
        cost_estimate=pl.CostEstimate(
            flops=2 * height * out_width * per_pixel, bytes_accessed=15 * 2 ** 20, transcendentals=0
        ),
        compiler_params=pltpu.CompilerParams(
            collective_id=0, has_side_effects=True, vmem_limit_bytes=52 * 2 ** 20
        ),
    )(assignment, features, w_reduce, w_expand, w_short, w_branch, w_dilated)
    return jnp.maximum(summed, jnp.zeros((), bf16))


def solution(mesh):
    in_specs = (
        P(("groups", "row"), "col", None, None),
        P(("groups", "row"), "col"),
        P(),
        P(),
        P(),
        P(),
        P(),
    )
    out_specs = P(("groups", "row"), "col", None)
    return jax.shard_map(
        functools.partial(shards, mesh.shape["row"], mesh.shape["col"]),
        mesh=mesh, in_specs=in_specs, out_specs=out_specs, check_vma=False,
    )
```
